32 devices in a mesh: seq: 8 (over y, x, core), head: 4 (over z).
Axes of the slice: x: 2, y: 2, z: 4, core: 2. Of those that a mesh axis runs over, the one named last changes fastest.
Arguments:
- queries: bfloat16 [4096, 4096], P(('seq', 'head')), may hold values from -6 to 6
- keys: bfloat16 [4096, 4096], P(('seq', 'head')), may hold values from -6 to 6
- values: bfloat16 [4096, 4096], P(('seq', 'head')), may hold values from -6 to 6
- beta: bfloat16 [4096, 32], P(('seq', 'head')), may hold values from 0 to 1
- log_decay: bfloat16 [4096, 32], P(('seq', 'head')), may hold values from -1 to 0
- seg_lengths: int32 [8], replicated, may hold values from 1 to 3072, 4096 in all
Outputs:
- mixed: bfloat16 [4096, 4096], P(('seq', 'head'))
The draws below stay inside these ranges and needn't reach their ends.
All inputs are finite; a program needn't handle non-finite values.
Results may differ from the reference program's by a relative error of at most 0.0017.
Values may be sent and summed in bfloat16 or wider, within the bound.
A program may use at most 128 MiB of HBM per device.

```python
import math
from functools import partial
import jax
import jax.numpy as jnp
import numpy as np
from jax import lax

H = 32
DK = 128
DV = 128
SPAN = 64
NSEG = 8
TOK_DEV = 128
PACKED_TOKENS = 4096


def head_decay_slowness(key, share):
    pick = jax.random.uniform(jax.random.fold_in(key, 11), (H,))
    slow_part = jax.random.uniform(jax.random.fold_in(key, 12), (H,), minval=0.85, maxval=1.0)
    fast_part = jax.random.uniform(jax.random.fold_in(key, 13), (H,), minval=0.0, maxval=0.6)
    return jnp.where(pick < share, slow_part, fast_part)


def draw_keys(key, part):
    key = jax.random.fold_in(key, 5)
    count = PACKED_TOKENS // SPAN
    direction = jax.random.normal(jax.random.fold_in(key, 1), (count, 1, H, DK), dtype=jnp.float32)
    lean = 2.0
    noise = jax.random.normal(jax.random.fold_in(key, 2), (count, SPAN, H, DK), dtype=jnp.float32)
    rows = jnp.clip(lean * direction + noise, -6.0, 6.0)
    return rows.reshape(PACKED_TOKENS, H * DK).astype(jnp.bfloat16)


def draw_log_decay(key, part):
    share = 0.5
    slowness = head_decay_slowness(key, share)
    log_rate = (1.0 - slowness) * math.log(1.0 / 40.0) + slowness * math.log(0.5 / PACKED_TOKENS)
    rough = jax.random.uniform(jax.random.fold_in(key, 21), (PACKED_TOKENS, H), minval=-0.7, maxval=0.7)
    blocky = jax.random.uniform(jax.random.fold_in(key, 22), (PACKED_TOKENS // TOK_DEV, H), minval=-0.7, maxval=0.7)
    blocky = jnp.repeat(blocky, TOK_DEV, axis=0)
    rate = jnp.exp(log_rate[None, :] + rough + blocky)
    segment_start_flags = jax.random.randint(jax.random.fold_in(key, 23), (8,), 0, PACKED_TOKENS)
    reset_hit_mask = jnp.any(jnp.arange(PACKED_TOKENS)[:, None] == segment_start_flags[None, :], axis=1)
    loss = jax.random.uniform(jax.random.fold_in(key, 24), (PACKED_TOKENS, H), minval=math.log(0.5), maxval=math.log(0.8))
    return (-rate + jnp.where(reset_hit_mask[:, None], loss, 0.0)).astype(jnp.bfloat16)


def draw_beta(key, part):
    share = 0.5
    slowness = head_decay_slowness(key, share)
    log_base = (1.0 - slowness) * math.log(0.5) + slowness * math.log(min(64.0 / PACKED_TOKENS, 0.5))
    rough = jax.random.uniform(jax.random.fold_in(key, 31), (PACKED_TOKENS, H), minval=-0.6, maxval=0.6)
    return jnp.exp(log_base[None, :] + rough).astype(jnp.bfloat16)


def levels(own_key, dims, cuts, low, high):
    factor_of = 1.0
    for position, shards_of in cuts:
        steps = jax.random.uniform(jax.random.fold_in(jax.random.fold_in(own_key, 6), position), (shards_of,), jnp.float32, low / len(cuts), high / len(cuts))
        factor_of = factor_of * jnp.repeat(jnp.exp(steps), dims[position] // shards_of).reshape((-1,) + (1,) * (len(dims) - 1 - position))
    return factor_of


def split_up(count, total, limit, skew):
    portions = [(1 << 20) // math.isqrt(grade ** skew) + 1 for grade in range(2, count + 1)]
    spare, counts = total - limit - (count - 1), [1] * (count - 1)
    while spare > 0:
        candidates = [i for i in range(count - 1) if counts[i] < limit]
        whole, remaining = sum([portions[i] for i in candidates]), spare
        for i in candidates:
            addition = min(limit - counts[i], max(1, remaining * portions[i] // whole), spare)
            counts[i] = counts[i] + addition
            spare = spare - addition
    return np.array([limit] + counts)


def ragged_sizes(stream_key, count, total, reach, slope):
    if count == 2:
        one = jax.random.randint(stream_key, (), max(1, total - reach), min(reach, total - 1) + 1)
        return jnp.stack([one, total - one])
    lengths = jnp.asarray(split_up(count, total, reach, slope), jnp.int32)
    twos = (count - 1) // 2
    source_of, receiver = lengths[1:1 + 2 * twos:2], lengths[2:2 + 2 * twos:2]
    room = jnp.minimum(source_of - 1, reach - receiver)
    moved = jax.random.randint(jax.random.fold_in(stream_key, 1), (twos,), 0, 1 << 20) % (room + 1)
    lengths = lengths.at[1:1 + 2 * twos:2].set(source_of - moved).at[2:2 + 2 * twos:2].set(receiver + moved)
    return lengths[jax.random.permutation(jax.random.fold_in(stream_key, 2), count)]


def normal_values(rng, shape, scale, reach, shards=(), kind=jnp.bfloat16):
    values = jax.random.normal(rng, shape, jnp.float32) * scale
    if len(shards) > 0:
        values = levels(rng, shape, shards, -0.22, 0.18) * values
    return jnp.clip(values, min=-reach, max=reach).astype(kind)


def setup_inputs(seed: int = 0) -> dict:
    splits = jax.random.split(jax.random.key(seed), 7)
    queries = normal_values(splits[0], (PACKED_TOKENS, H * DK), 1.0, 6.0, ((0, 32),))
    keys = draw_keys(jax.random.fold_in(splits[6], 71), 0)
    values = normal_values(splits[2], (PACKED_TOKENS, H * DV), 1.0, 6.0, ((0, 32),))
    beta = draw_beta(jax.random.fold_in(splits[6], 71), 0)
    log_decay = draw_log_decay(jax.random.fold_in(splits[6], 71), 0)
    seg_lengths = ragged_sizes(splits[5], NSEG, PACKED_TOKENS, PACKED_TOKENS * 3 // 4, 2).astype(jnp.int32)
    return dict(queries=queries, keys=keys, values=values, beta=beta, log_decay=log_decay, seg_lengths=seg_lengths)


def span_parts(query_rows, key_rows, value_rows, write_rate, log_gate, reset_flags, inclusive):
    highest = lax.Precision.HIGHEST
    block_rows = query_rows.shape[0]
    log_level = jnp.cumsum(log_gate)
    region = jnp.cumsum(reset_flags)
    row_indices = jnp.arange(block_rows)[:, None]
    col_ids = jnp.arange(block_rows)[None, :]
    inside_segment_mask = (col_ids <= row_indices) & (region[:, None] == region[None, :])
    log_gap = jnp.where(inside_segment_mask, log_level[:, None] - log_level[None, :], 0.0)
    weight = jnp.where(inside_segment_mask, jnp.exp(log_gap), 0.0)
    carried = jnp.where(region == 0, jnp.exp(log_level), 0.0)
    strictly = col_ids < row_indices
    intersection = jnp.dot(key_rows, key_rows.T, precision=highest)
    system = jnp.eye(block_rows, dtype=query_rows.dtype) + jnp.where(strictly, write_rate[:, None] * weight * intersection, 0.0)
    right_side = jnp.concatenate([write_rate[:, None] * value_rows, (write_rate * carried)[:, None] * key_rows], axis=1)
    solved = lax.linalg.triangular_solve(system, right_side, left_side=True, lower=True, unit_diagonal=True)
    value_width = value_rows.shape[1]
    update = solved[:, :value_width]
    shrink = solved[:, value_width:]
    scores = jnp.dot(query_rows, key_rows.T, precision=highest) * weight
    if not inclusive:
        scores = jnp.where(strictly, scores, 0.0)
    local_out = jnp.dot(scores, update, precision=highest)
    effective = carried[:, None] * query_rows - jnp.dot(scores, shrink, precision=highest)
    trailing_weight = weight[block_rows - 1]
    scaled = trailing_weight[:, None] * key_rows
    transit = carried[block_rows - 1] * jnp.eye(key_rows.shape[1], dtype=query_rows.dtype) - jnp.dot(shrink.T, scaled, precision=highest)
    inject = jnp.dot(update.T, scaled, precision=highest)
    return (local_out, effective, transit, inject)

def block_pieces(query_rows, key_rows, value_rows, write_rate, log_gate, reset_flags, inclusive):
    count = query_rows.shape[0] // SPAN

    def split(member):
        return member.reshape((count, SPAN) + member.shape[1:])
    return jax.vmap(partial(span_parts, inclusive=inclusive))(split(query_rows), split(key_rows), split(value_rows), split(write_rate), split(log_gate), split(reset_flags))

def run_direction(query_rows, key_rows, value_rows, write_rate, log_gate, reset_flags, inclusive):
    highest = lax.Precision.HIGHEST
    pieces = block_pieces(query_rows, key_rows, value_rows, write_rate, log_gate, reset_flags, inclusive)
    start = jnp.zeros((value_rows.shape[1], key_rows.shape[1]), query_rows.dtype)

    def advance(state, piece):
        out_block, effect_rows, transit_step, inject_step = piece
        produced = out_block + jnp.dot(effect_rows, state.T, precision=highest)
        return (jnp.dot(state, transit_step, precision=highest) + inject_step, produced)
    final_state, outputs = lax.scan(advance, start, pieces)
    return outputs.reshape(-1, value_rows.shape[1])

def reference(queries, keys, values, beta, log_decay, seg_lengths):
    total = queries.shape[0]
    starts = (jnp.cumsum(seg_lengths) - seg_lengths).astype(jnp.int32)
    positions = jnp.arange(total, dtype=jnp.int32)
    forward_reset = jnp.any(positions[:, None] == starts[None, :], axis=1).astype(jnp.int32)
    backward_reset = (jnp.any((positions + 1)[:, None] == starts[None, :], axis=1) | (positions == total - 1)).astype(jnp.int32)

    def by_head(array, width):
        return array.reshape(total, H, width).transpose(1, 0, 2)
    head_data = (by_head(queries, DK), by_head(keys, DK), by_head(values, DV), beta.T, log_decay.T)

    def one_head(member):
        query_rows = member[0].astype(jnp.float32)
        key_raw = member[1].astype(jnp.float32)
        value_rows = member[2].astype(jnp.float32)
        write_rate = member[3].astype(jnp.float32)
        log_gate = member[4].astype(jnp.float32)
        key_rows = key_raw / jnp.sqrt(lax.optimization_barrier(jnp.sum(key_raw * key_raw, axis=-1, keepdims=True)) + 1e-06)
        forward = run_direction(query_rows, key_rows, value_rows, write_rate, log_gate, forward_reset, True)
        backward = run_direction(query_rows[::-1], key_rows[::-1], value_rows[::-1], write_rate[::-1], log_gate[::-1], backward_reset[::-1], False)[::-1]
        return forward + backward
    outputs = lax.map(one_head, head_data)
    return outputs.transpose(1, 0, 2).reshape(total, H * DV).astype(jnp.bfloat16)
```

```python
from functools import partial

import jax
import jax.numpy as jnp
from jax import lax
from jax.experimental import pallas as pl
from jax.experimental.pallas import tpu as pltpu
from jax.sharding import PartitionSpec as P

DK = 128
DV = 128
SPAN = 64
TILE = 128
SIDE = 16
GROUP = 4
LEVELS = 6


def mm(a, b):
    return jnp.dot(a, b, preferred_element_type=jnp.float32)


def halves(a):
    high = a.astype(jnp.bfloat16)
    low = (a - high.astype(jnp.float32)).astype(jnp.bfloat16)
    return high, low


def wide(a):
    return jnp.concatenate(halves(a), axis=1)


def right(high, low):
    row = jnp.concatenate([high, low], axis=1)
    return jnp.concatenate([row, row], axis=0)


def fold(a):
    return a[:, :TILE] + a[:, TILE:]


def mix_kernel(count, group, lengths, x_ref, out_ref, masks, fe, go, partial_out):
    bf16, f32 = jnp.bfloat16, jnp.float32
    rows = lax.broadcasted_iota(jnp.int32, (TILE, TILE), 0)
    cols = lax.broadcasted_iota(jnp.int32, (TILE, TILE), 1)
    rows_w = lax.broadcasted_iota(jnp.int32, (TILE, 2 * TILE), 0)
    cols_w = lax.broadcasted_iota(jnp.int32, (TILE, 2 * TILE), 1) & (TILE - 1)
    for level in range(1, LEVELS + 1):
        hit = ((rows_w ^ cols_w) >> level) == 1
        masks[level - 1] = jnp.where(hit, 1.0, 0.0).astype(f32).astype(bf16)
    starts = []
    total = jnp.int32(0)
    for s in range(lengths.shape[0]):
        starts.append(total)
        total = total + lengths[s]

    def segment_of(position):
        seg = jnp.zeros_like(position)
        for s in starts:
            seg = seg + jnp.where(position >= s, 1, 0)
        return seg

    def prepare(g, carry):
        eye = jnp.where(rows == cols, 1.0, 0.0).astype(f32)
        ramp = jnp.where(rows <= cols, 1.0, 0.0).astype(f32).astype(bf16)
        near = (rows ^ cols) == 1
        chains = []
        for m in range(group):
            c = g * group + m
            q = x_ref[c, 0:TILE, :]
            k = x_ref[c, TILE : 2 * TILE, :]
            v = x_ref[c, 2 * TILE : 3 * TILE, :]
            side = x_ref[c, 3 * TILE : 3 * TILE + SIDE, :]
            k_t = k.astype(f32).T.astype(bf16)
            both = mm(jnp.concatenate([q, k], axis=0), k_t)
            qk, kk = both[:TILE], both[TILE:]
            level = mm(side, ramp)
            side32 = side.astype(f32)
            b_row, g_row = side32[0:1], side32[1:2]
            inc_row = level[1:2]
            exc_row = inc_row - g_row
            base = c * TILE
            position = base + lax.broadcasted_iota(jnp.int32, (1, TILE), 1)
            seg_row = segment_of(position).astype(f32)
            before = segment_of(base - 1).astype(f32)
            after = jnp.where(c == count - 1, -1, segment_of(base + TILE)).astype(f32)
            stacked = jnp.concatenate(
                [inc_row, exc_row, b_row, seg_row, jnp.zeros((4, TILE), f32)], axis=0
            )
            stacked_t = stacked.T
            inc_col, exc_col = stacked_t[:, 0:1], stacked_t[:, 1:2]
            b_col, seg_col = stacked_t[:, 2:3], stacked_t[:, 3:4]
            diagonal = kk * eye
            rn_row = 1.0 / jnp.sqrt(jnp.sum(diagonal, axis=0, keepdims=True) + 1e-06)
            rn_col = 1.0 / jnp.sqrt(jnp.sum(diagonal, axis=1, keepdims=True) + 1e-06)
            same = seg_col == seg_row
            kk_b = kk * (rn_col * b_col) * rn_row
            qk_n = qk * rn_row
            last_inc = inc_row[:, TILE - 1 : TILE]
            last_seg = seg_row[:, TILE - 1 : TILE]
            first_seg = seg_row[:, 0:1]
            v2 = jnp.concatenate([v, v], axis=0)
            k2 = jnp.concatenate([k, k], axis=0)
            kt2 = jnp.concatenate([k_t, k_t], axis=1)
            q32 = q.astype(f32)
            for direction in range(2):
                if direction == 0:
                    inside = same & (cols <= rows)
                    strict = cols < rows
                    gap = inc_col - inc_row
                    c_row = jnp.where(seg_row == before, jnp.exp(inc_row), 0.0)
                    c_col = jnp.where(seg_col == before, jnp.exp(inc_col), 0.0)
                    w_col = jnp.where(seg_col == last_seg, jnp.exp(last_inc - inc_col), 0.0)
                    c_last = c_row[:, TILE - 1 : TILE]
                else:
                    inside = same & (cols >= rows)
                    strict = cols > rows
                    gap = exc_row - exc_col
                    c_row = jnp.where(seg_row == after, jnp.exp(last_inc - exc_row), 0.0)
                    c_col = jnp.where(seg_col == after, jnp.exp(last_inc - exc_col), 0.0)
                    w_col = jnp.where(seg_col == first_seg, jnp.exp(exc_col), 0.0)
                    c_last = c_row[:, 0:1]
                weight = jnp.where(inside, jnp.exp(jnp.where(inside, gap, 0.0)), 0.0)
                lower = jnp.where(strict, weight * kk_b, 0.0)
                scores = weight * qk_n
                if direction == 1:
                    scores = jnp.where(strict, scores, 0.0)
                chains.append(
                    dict(
                        place=2 * c + direction,
                        lower=wide(lower),
                        inverse=eye - jnp.where(near, lower, 0.0),
                        scores=halves(scores),
                        b_row=b_row,
                        bc_row=b_row * c_row * rn_row,
                        wn_col=w_col * rn_col,
                        c_last=c_last,
                        cq=c_col * q32,
                        v2=v2,
                        k2=k2,
                        kt2=kt2,
                    )
                )
        for level in range(LEVELS):
            mask = masks[level]
            parts = [halves(n["inverse"]) for n in chains]
            inner = [fold(mm(n["lower"] * mask, right(*p))) for n, p in zip(chains, parts)]
            outer = [
                fold(mm(jnp.concatenate(p, axis=1), right(*halves(y))))
                for p, y in zip(parts, inner)
            ]
            for n, y in zip(chains, outer):
                n["inverse"] = n["inverse"] - y
        solved = [
            jnp.concatenate(
                [
                    mm(wide(n["inverse"] * n["b_row"]), n["v2"]),
                    mm(wide(n["inverse"] * n["bc_row"]), n["k2"]),
                ],
                axis=1,
            )
            for n in chains
        ]
        for n, u in zip(chains, solved):
            u_h, u_l = halves(u)
            s_h, s_l = n["scores"]
            seen = mm(jnp.concatenate([s_h, s_l], axis=1), jnp.concatenate([u_h, u_h], axis=0))
            seen = seen + mm(s_h, u_l)
            kept = mm(n["kt2"], jnp.concatenate(halves(u * n["wn_col"]), axis=0))
            effect = n["cq"] - seen[:, TILE:]
            transit = n["c_last"] * eye - kept[:, TILE:]
            fe[n["place"]] = wide(jnp.concatenate([transit, effect], axis=0))
            go[n["place"]] = jnp.concatenate([kept[:, :TILE], seen[:, :TILE]], axis=0)
        return carry

    lax.fori_loop(0, count // group, prepare, 0)

    def advance(step, states):
        later = []
        for direction, state in enumerate(states):
            c = step if direction == 0 else count - 1 - step
            place = 2 * c + direction
            moved = fold(mm(fe[place], right(*halves(state)))) + go[place]
            partial_out[place] = moved[TILE:]
            later.append(moved[:TILE])
        return tuple(later)

    empty = jnp.zeros((TILE, TILE), f32)
    lax.fori_loop(0, count, advance, (empty, empty))

    def finish(c, carry):
        out_ref[c] = (partial_out[2 * c] + partial_out[2 * c + 1]).astype(bf16)
        return carry

    lax.fori_loop(0, count, finish, 0)


def mix_head(x, seg_lengths):
    count = x.shape[0]
    group = GROUP if count % GROUP == 0 else 1
    return pl.pallas_call(
        partial(mix_kernel, count, group),
        out_shape=jax.ShapeDtypeStruct((count, TILE, DV), jnp.bfloat16),
        in_specs=[
            pl.BlockSpec(memory_space=pltpu.SMEM),
            pl.BlockSpec(memory_space=pltpu.VMEM),
        ],
        out_specs=pl.BlockSpec(memory_space=pltpu.VMEM),
        scratch_shapes=[
            pltpu.VMEM((LEVELS, TILE, 2 * TILE), jnp.bfloat16),
            pltpu.VMEM((2 * count, 2 * TILE, 2 * TILE), jnp.bfloat16),
            pltpu.VMEM((2 * count, 2 * TILE, TILE), jnp.float32),
            pltpu.VMEM((2 * count, TILE, TILE), jnp.float32),
        ],
        compiler_params=pltpu.CompilerParams(vmem_limit_bytes=52 * 1024 * 1024),
        cost_estimate=pl.CostEstimate(
            flops=count * 40 * TILE * 512 * 256, bytes_accessed=count * 131072, transcendentals=0
        ),
    )(seg_lengths, x)


def one_head_each(queries, keys, values, beta, log_decay, seg_lengths):
    axes = ("seq", "head")
    tokens = queries.shape[0]
    heads = beta.shape[1]

    def by_head(array):
        return array.reshape(tokens, heads, TILE).transpose(1, 0, 2)

    side = jnp.stack([beta.T, log_decay.T], axis=1)
    side = jnp.pad(side, ((0, 0), (0, SIDE - 2), (0, 0)))
    packed = jnp.concatenate([by_head(queries), by_head(keys), by_head(values), side], axis=1)
    x = lax.all_to_all(packed, axes, split_axis=0, concat_axis=0, tiled=True)
    mixed = mix_head(x, seg_lengths)
    back = lax.all_to_all(mixed, axes, split_axis=0, concat_axis=0, tiled=True)
    return back.transpose(1, 0, 2).reshape(tokens, heads * DV)


def span_parts(query_rows, key_rows, value_rows, write_rate, log_gate, reset_flags, inclusive):
    highest = lax.Precision.HIGHEST
    block_rows = query_rows.shape[0]
    log_level = jnp.cumsum(log_gate)
    region = jnp.cumsum(reset_flags)
    row_indices = jnp.arange(block_rows)[:, None]
    col_ids = jnp.arange(block_rows)[None, :]
    inside_segment_mask = (col_ids <= row_indices) & (region[:, None] == region[None, :])
    log_gap = jnp.where(inside_segment_mask, log_level[:, None] - log_level[None, :], 0.0)
    weight = jnp.where(inside_segment_mask, jnp.exp(log_gap), 0.0)
    carried = jnp.where(region == 0, jnp.exp(log_level), 0.0)
    strictly = col_ids < row_indices
    intersection = jnp.dot(key_rows, key_rows.T, precision=highest)
    system = jnp.eye(block_rows, dtype=query_rows.dtype) + jnp.where(
        strictly, write_rate[:, None] * weight * intersection, 0.0
    )
    right_side = jnp.concatenate(
        [write_rate[:, None] * value_rows, (write_rate * carried)[:, None] * key_rows], axis=1
    )
    solved = jax.scipy.linalg.solve_triangular(system, right_side, lower=True, unit_diagonal=True)
    value_width = value_rows.shape[1]
    update = solved[:, :value_width]
    shrink = solved[:, value_width:]
    scores = jnp.dot(query_rows, key_rows.T, precision=highest) * weight
    if not inclusive:
        scores = jnp.where(strictly, scores, 0.0)
    local_out = jnp.dot(scores, update, precision=highest)
    effective = carried[:, None] * query_rows - jnp.dot(scores, shrink, precision=highest)
    trailing_weight = weight[block_rows - 1]
    scaled = trailing_weight[:, None] * key_rows
    transit = carried[block_rows - 1] * jnp.eye(
        key_rows.shape[1], dtype=query_rows.dtype
    ) - jnp.dot(shrink.T, scaled, precision=highest)
    inject = jnp.dot(update.T, scaled, precision=highest)
    return (local_out, effective, transit, inject)


def block_pieces(query_rows, key_rows, value_rows, write_rate, log_gate, reset_flags, inclusive):
    count = query_rows.shape[0] // SPAN

    def split(member):
        return member.reshape((count, SPAN) + member.shape[1:])

    return jax.vmap(partial(span_parts, inclusive=inclusive))(
        split(query_rows),
        split(key_rows),
        split(value_rows),
        split(write_rate),
        split(log_gate),
        split(reset_flags),
    )


def combine(earlier, later):
    highest = lax.Precision.HIGHEST
    return (
        jnp.einsum("hij,hjk->hik", earlier[0], later[0], precision=highest),
        jnp.einsum("hij,hjk->hik", earlier[1], later[0], precision=highest) + later[1],
    )


def summarize(transit, inject):
    heads = transit.shape[0]
    start = (
        jnp.broadcast_to(jnp.eye(DK, dtype=jnp.float32), (heads, DK, DK)),
        jnp.zeros((heads, DV, DK), jnp.float32),
    )

    def step(carry, piece):
        return (combine(carry, piece), None)

    result, unused = lax.scan(
        step, start, (jnp.moveaxis(transit, 1, 0), jnp.moveaxis(inject, 1, 0))
    )
    return result


def emit(local_out, effective, transit, inject, state):
    highest = lax.Precision.HIGHEST
    moved = (
        jnp.moveaxis(local_out, 1, 0),
        jnp.moveaxis(effective, 1, 0),
        jnp.moveaxis(transit, 1, 0),
        jnp.moveaxis(inject, 1, 0),
    )

    def step(carry, piece):
        out_block, effect_rows, transit_step, inject_step = piece
        produced = out_block + jnp.einsum("hck,hvk->hcv", effect_rows, carry, precision=highest)
        carry = jnp.einsum("hvj,hjk->hvk", carry, transit_step, precision=highest) + inject_step
        return (carry, produced)

    final_state, produced = lax.scan(step, state, moved)
    heads = produced.shape[1]
    return jnp.moveaxis(produced, 0, 1).reshape(heads, -1, produced.shape[-1])


def on_device(queries, keys, values, beta, log_decay, seg_lengths):
    highest = lax.Precision.HIGHEST
    query_all, key_all, value_all, rate_all, gate_values_full = (
        lax.all_to_all(queries, "head", split_axis=1, concat_axis=0, tiled=True),
        lax.all_to_all(keys, "head", split_axis=1, concat_axis=0, tiled=True),
        lax.all_to_all(values, "head", split_axis=1, concat_axis=0, tiled=True),
        lax.all_to_all(beta, "head", split_axis=1, concat_axis=0, tiled=True),
        lax.all_to_all(log_decay, "head", split_axis=1, concat_axis=0, tiled=True),
    )
    rows = query_all.shape[0]
    heads = rate_all.shape[1]
    spread = lax.axis_size("seq")
    place = lax.axis_index("seq")
    total = rows * spread
    starts = jnp.cumsum(seg_lengths) - seg_lengths
    positions = place * rows + jnp.arange(rows, dtype=jnp.int32)
    forward_reset = jnp.any(positions[:, None] == starts[None, :], axis=1).astype(jnp.int32)
    backward_reset = (
        jnp.any((positions + 1)[:, None] == starts[None, :], axis=1) | (positions == total - 1)
    ).astype(jnp.int32)

    def by_head(array, width):
        return array.reshape(rows, heads, width).transpose(1, 0, 2).astype(jnp.float32)

    query_heads = by_head(query_all, DK)
    key_raw = by_head(key_all, DK)
    key_heads = key_raw / jnp.sqrt(jnp.sum(key_raw * key_raw, axis=-1, keepdims=True) + 1e-06)
    value_heads = by_head(value_all, DV)
    rate_heads = rate_all.T.astype(jnp.float32)
    gate_heads = gate_values_full.T.astype(jnp.float32)
    forward_pieces = jax.vmap(partial(block_pieces, reset_flags=forward_reset, inclusive=True))(
        query_heads, key_heads, value_heads, rate_heads, gate_heads
    )
    backward_pieces = jax.vmap(
        partial(block_pieces, reset_flags=backward_reset[::-1], inclusive=False)
    )(
        query_heads[:, ::-1],
        key_heads[:, ::-1],
        value_heads[:, ::-1],
        rate_heads[:, ::-1],
        gate_heads[:, ::-1],
    )
    forward_sum = summarize(forward_pieces[2], forward_pieces[3])
    backward_sum = summarize(backward_pieces[2], backward_pieces[3])
    every = (
        lax.all_gather(forward_sum[0][None], "seq", axis=0, tiled=True),
        lax.all_gather(forward_sum[1][None], "seq", axis=0, tiled=True),
        lax.all_gather(backward_sum[0][None], "seq", axis=0, tiled=True),
        lax.all_gather(backward_sum[1][None], "seq", axis=0, tiled=True),
    )
    empty = jnp.zeros_like(forward_sum[1])

    def take_lower(step, state):
        moved = (
            jnp.einsum("hvj,hjk->hvk", state, every[0][step], precision=highest) + every[1][step]
        )
        return jnp.where(step < place, moved, state)

    def take_upper(step, state):
        source = spread - 1 - step
        moved = (
            jnp.einsum("hvj,hjk->hvk", state, every[2][source], precision=highest)
            + every[3][source]
        )
        return jnp.where(source > place, moved, state)

    forward_in = lax.fori_loop(0, spread, take_lower, empty)
    backward_in = lax.fori_loop(0, spread, take_upper, empty)
    forward_out = emit(
        forward_pieces[0], forward_pieces[1], forward_pieces[2], forward_pieces[3], forward_in
    )
    backward_out = emit(
        backward_pieces[0], backward_pieces[1], backward_pieces[2], backward_pieces[3], backward_in
    )[:, ::-1]
    mixed = (
        (forward_out + backward_out)
        .transpose(1, 0, 2)
        .reshape(rows, heads * DV)
        .astype(jnp.bfloat16)
    )
    return lax.all_to_all(mixed, "head", split_axis=0, concat_axis=1, tiled=True)


def solution(mesh):
    in_specs = (
        P(("seq", "head"), None),
        P(("seq", "head"), None),
        P(("seq", "head"), None),
        P(("seq", "head"), None),
        P(("seq", "head"), None),
        P(),
    )
    out_specs = P(("seq", "head"), None)
    devices = mesh.shape["seq"] * mesh.shape["head"]

    def run(queries, keys, values, beta, log_decay, seg_lengths):
        alone = beta.shape[1] == devices and queries.shape[0] == devices * TILE
        return jax.shard_map(
            one_head_each if alone else on_device,
            mesh=mesh,
            in_specs=in_specs,
            out_specs=out_specs,
            check_vma=False,
        )(queries, keys, values, beta, log_decay, seg_lengths)

    return run
```

```python
from functools import partial

import jax
import jax.numpy as jnp
from jax import lax
from jax.experimental import pallas as pl
from jax.experimental.pallas import tpu as pltpu
from jax.sharding import PartitionSpec as P

DK = 128
DV = 128
SPAN = 64
TILE = 128
SIDE = 16
GROUP = 4
LEVELS = 6


def mm(a, b):
    return jnp.dot(a, b, preferred_element_type=jnp.float32)


def halves(a):
    high = a.astype(jnp.bfloat16)
    low = (a - high.astype(jnp.float32)).astype(jnp.bfloat16)
    return high, low


def wide(a):
    return jnp.concatenate(halves(a), axis=1)


def right(high, low):
    row = jnp.concatenate([high, low], axis=1)
    return jnp.concatenate([row, row], axis=0)


def fold(a):
    return a[:, :TILE] + a[:, TILE:]


def mix_kernel(
    spread,
    inner,
    group,
    lengths,
    side_ref,
    q_ref,
    k_ref,
    v_ref,
    out_ref,
    q_all,
    k_all,
    v_all,
    side_all,
    masks,
    fe,
    go,
    partial_out,
    mixed,
    own_sem,
    send_sem,
    recv_sem,
    back_send,
    back_recv,
):
    count = spread * inner
    me = lax.axis_index("seq") * inner + lax.axis_index("head")

    def device(index):
        return (index // inner, index % inner)

    def columns(index):
        return pl.ds(pl.multiple_of(index * TILE, TILE), TILE)

    barrier = pltpu.get_barrier_semaphore()

    def greet(s, carry):
        pl.semaphore_signal(
            barrier,
            inc=1,
            device_id=device((me + s) % count),
            device_id_type=pl.DeviceIdType.MESH,
        )
        return carry

    lax.fori_loop(1, count, greet, 0)
    pl.semaphore_wait(barrier, count - 1)

    def pairs(head, block):
        return (
            (side_ref.at[head], side_all.at[block]),
            (k_ref.at[:, columns(head)], k_all.at[block]),
            (v_ref.at[:, columns(head)], v_all.at[block]),
            (q_ref.at[:, columns(head)], q_all.at[block]),
        )

    def sends(target, source):
        return [
            pltpu.make_async_remote_copy(
                src_ref=src,
                dst_ref=dst,
                send_sem=send_sem.at[kind, target],
                recv_sem=recv_sem.at[kind, source],
                device_id=device(target),
                device_id_type=pl.DeviceIdType.MESH,
            )
            for kind, (src, dst) in enumerate(pairs(target, source))
        ]

    def give(s, carry):
        for copy in sends((me + s) % count, me):
            copy.start()
        return carry

    lax.fori_loop(1, count, give, 0)
    own = [
        pltpu.make_async_copy(src, dst, own_sem.at[kind])
        for kind, (src, dst) in enumerate(pairs(me, me))
    ]
    for copy in own:
        copy.start()

    bf16, f32 = jnp.bfloat16, jnp.float32
    rows = lax.broadcasted_iota(jnp.int32, (TILE, TILE), 0)
    cols = lax.broadcasted_iota(jnp.int32, (TILE, TILE), 1)
    rows_w = lax.broadcasted_iota(jnp.int32, (TILE, 2 * TILE), 0)
    cols_w = lax.broadcasted_iota(jnp.int32, (TILE, 2 * TILE), 1) & (TILE - 1)
    for level in range(1, LEVELS + 1):
        hit = ((rows_w ^ cols_w) >> level) == 1
        masks[level - 1] = jnp.where(hit, 1.0, 0.0).astype(f32).astype(bf16)
    starts = []
    total = jnp.int32(0)
    for s in range(lengths.shape[0]):
        starts.append(total)
        total = total + lengths[s]

    def segment_of(position):
        seg = jnp.zeros_like(position)
        for s in starts:
            seg = seg + jnp.where(position >= s, 1, 0)
        return seg

    for copy in own:
        copy.wait()

    def prepare(g, carry):
        for m in range(group):
            s = g * group + m

            @pl.when(s > 0)
            def _():
                source = (me + count - s) % count
                for copy in sends(source, source):
                    copy.wait_recv()

        eye = jnp.where(rows == cols, 1.0, 0.0).astype(f32)
        ramp = jnp.where(rows <= cols, 1.0, 0.0).astype(f32).astype(bf16)
        near = (rows ^ cols) == 1
        chains = []
        for m in range(group):
            c = (me + count - (g * group + m)) % count
            q, k, v, side = q_all[c], k_all[c], v_all[c], side_all[c]
            k_t = k.astype(f32).T.astype(bf16)
            both = mm(jnp.concatenate([q, k], axis=0), k_t)
            qk, kk = both[:TILE], both[TILE:]
            level = mm(side, ramp)
            side32 = side.astype(f32)
            b_row, g_row = side32[0:1], side32[1:2]
            inc_row = level[1:2]
            exc_row = inc_row - g_row
            base = c * TILE
            position = base + lax.broadcasted_iota(jnp.int32, (1, TILE), 1)
            seg_row = segment_of(position).astype(f32)
            before = segment_of(base - 1).astype(f32)
            after = jnp.where(c == count - 1, -1, segment_of(base + TILE)).astype(f32)
            stacked = jnp.concatenate(
                [inc_row, exc_row, b_row, seg_row, jnp.zeros((4, TILE), f32)], axis=0
            )
            stacked_t = stacked.T
            inc_col, exc_col = stacked_t[:, 0:1], stacked_t[:, 1:2]
            b_col, seg_col = stacked_t[:, 2:3], stacked_t[:, 3:4]
            diagonal = kk * eye
            rn_row = 1.0 / jnp.sqrt(jnp.sum(diagonal, axis=0, keepdims=True) + 1e-06)
            rn_col = 1.0 / jnp.sqrt(jnp.sum(diagonal, axis=1, keepdims=True) + 1e-06)
            same = seg_col == seg_row
            kk_b = kk * (rn_col * b_col) * rn_row
            qk_n = qk * rn_row
            last_inc = inc_row[:, TILE - 1 : TILE]
            last_seg = seg_row[:, TILE - 1 : TILE]
            first_seg = seg_row[:, 0:1]
            v2 = jnp.concatenate([v, v], axis=0)
            k2 = jnp.concatenate([k, k], axis=0)
            kt2 = jnp.concatenate([k_t, k_t], axis=1)
            q32 = q.astype(f32)
            for direction in range(2):
                if direction == 0:
                    inside = same & (cols <= rows)
                    strict = cols < rows
                    gap = inc_col - inc_row
                    c_row = jnp.where(seg_row == before, jnp.exp(inc_row), 0.0)
                    c_col = jnp.where(seg_col == before, jnp.exp(inc_col), 0.0)
                    w_col = jnp.where(seg_col == last_seg, jnp.exp(last_inc - inc_col), 0.0)
                    c_last = c_row[:, TILE - 1 : TILE]
                else:
                    inside = same & (cols >= rows)
                    strict = cols > rows
                    gap = exc_row - exc_col
                    c_row = jnp.where(seg_row == after, jnp.exp(last_inc - exc_row), 0.0)
                    c_col = jnp.where(seg_col == after, jnp.exp(last_inc - exc_col), 0.0)
                    w_col = jnp.where(seg_col == first_seg, jnp.exp(exc_col), 0.0)
                    c_last = c_row[:, 0:1]
                weight = jnp.where(inside, jnp.exp(jnp.where(inside, gap, 0.0)), 0.0)
                lower = jnp.where(strict, weight * kk_b, 0.0)
                scores = weight * qk_n
                if direction == 1:
                    scores = jnp.where(strict, scores, 0.0)
                chains.append(
                    dict(
                        place=2 * c + direction,
                        lower=wide(lower),
                        inverse=eye - jnp.where(near, lower, 0.0),
                        scores=halves(scores),
                        b_row=b_row,
                        bc_row=b_row * c_row * rn_row,
                        wn_col=w_col * rn_col,
                        c_last=c_last,
                        cq=c_col * q32,
                        v2=v2,
                        k2=k2,
                        kt2=kt2,
                    )
                )
        for level in range(LEVELS):
            mask = masks[level]
            parts = [halves(n["inverse"]) for n in chains]
            inner = [fold(mm(n["lower"] * mask, right(*p))) for n, p in zip(chains, parts)]
            outer = [
                fold(mm(jnp.concatenate(p, axis=1), right(*halves(y))))
                for p, y in zip(parts, inner)
            ]
            for n, y in zip(chains, outer):
                n["inverse"] = n["inverse"] - y
        solved = [
            jnp.concatenate(
                [
                    mm(wide(n["inverse"] * n["b_row"]), n["v2"]),
                    mm(wide(n["inverse"] * n["bc_row"]), n["k2"]),
                ],
                axis=1,
            )
            for n in chains
        ]
        for n, u in zip(chains, solved):
            u_h, u_l = halves(u)
            s_h, s_l = n["scores"]
            seen = mm(jnp.concatenate([s_h, s_l], axis=1), jnp.concatenate([u_h, u_h], axis=0))
            seen = seen + mm(s_h, u_l)
            kept = mm(n["kt2"], jnp.concatenate(halves(u * n["wn_col"]), axis=0))
            effect = n["cq"] - seen[:, TILE:]
            transit = n["c_last"] * eye - kept[:, TILE:]
            fe[n["place"]] = wide(jnp.concatenate([transit, effect], axis=0))
            go[n["place"]] = jnp.concatenate([kept[:, :TILE], seen[:, :TILE]], axis=0)
        return carry

    lax.fori_loop(0, count // group, prepare, 0)

    def advance(turn, states):
        for m in range(group):
            step = turn * group + m
            later = []
            for direction, state in enumerate(states):
                c = step if direction == 0 else count - 1 - step
                place = 2 * c + direction
                moved = fold(mm(fe[place], right(*halves(state)))) + go[place]
                partial_out[place] = moved[TILE:]
                later.append(moved[:TILE])
            states = tuple(later)
        return states

    empty = jnp.zeros((TILE, TILE), f32)
    lax.fori_loop(0, count // group, advance, (empty, empty))

    def returns(target, source):
        return pltpu.make_async_remote_copy(
            src_ref=mixed.at[target],
            dst_ref=out_ref.at[:, columns(source)],
            send_sem=back_send.at[target],
            recv_sem=back_recv.at[source],
            device_id=device(target),
            device_id_type=pl.DeviceIdType.MESH,
        )

    def finish(s, carry):
        c = (me + s) % count
        mixed[c] = (partial_out[2 * c] + partial_out[2 * c + 1]).astype(bf16)
        returns(c, me).start()
        return carry

    lax.fori_loop(1, count, finish, 0)
    out_ref[:, columns(me)] = (partial_out[2 * me] + partial_out[2 * me + 1]).astype(bf16)

    def settle(s, carry):
        target = (me + s) % count
        for copy in sends(target, me):
            copy.wait_send()
        returns(target, me).wait_send()
        source = (me + count - s) % count
        returns(source, source).wait_recv()
        return carry

    lax.fori_loop(1, count, settle, 0)


def one_head_each(queries, keys, values, beta, log_decay, seg_lengths):
    spread, inner = lax.axis_size("seq"), lax.axis_size("head")
    count = spread * inner
    group = GROUP if count % GROUP == 0 else 1
    side = jnp.stack([beta.T, log_decay.T], axis=1)
    side = jnp.pad(side, ((0, 0), (0, SIDE - 2), (0, 0)))
    return pl.pallas_call(
        partial(mix_kernel, spread, inner, group),
        out_shape=jax.ShapeDtypeStruct((TILE, count * DV), jnp.bfloat16),
        in_specs=[pl.BlockSpec(memory_space=pltpu.SMEM)]
        + [pl.BlockSpec(memory_space=pltpu.VMEM)]
        + [pl.BlockSpec(memory_space=pl.ANY)] * 3,
        out_specs=pl.BlockSpec(memory_space=pltpu.VMEM),
        scratch_shapes=[
            pltpu.VMEM((count, TILE, DK), jnp.bfloat16),
            pltpu.VMEM((count, TILE, DK), jnp.bfloat16),
            pltpu.VMEM((count, TILE, DV), jnp.bfloat16),
            pltpu.VMEM((count, SIDE, TILE), jnp.bfloat16),
            pltpu.VMEM((LEVELS, TILE, 2 * TILE), jnp.bfloat16),
            pltpu.VMEM((2 * count, 2 * TILE, 2 * TILE), jnp.bfloat16),
            pltpu.VMEM((2 * count, 2 * TILE, TILE), jnp.float32),
            pltpu.VMEM((2 * count, TILE, TILE), jnp.float32),
            pltpu.VMEM((count, TILE, DV), jnp.bfloat16),
            pltpu.SemaphoreType.DMA((4,)),
            pltpu.SemaphoreType.DMA((4, count)),
            pltpu.SemaphoreType.DMA((4, count)),
            pltpu.SemaphoreType.DMA((count,)),
            pltpu.SemaphoreType.DMA((count,)),
        ],
        compiler_params=pltpu.CompilerParams(
            collective_id=0, has_side_effects=True, vmem_limit_bytes=52 * 1024 * 1024
        ),
        cost_estimate=pl.CostEstimate(
            flops=count * 40 * TILE * 512 * 256, bytes_accessed=count * 131072, transcendentals=0
        ),
    )(seg_lengths, side, queries, keys, values)


def span_parts(query_rows, key_rows, value_rows, write_rate, log_gate, reset_flags, inclusive):
    highest = lax.Precision.HIGHEST
    block_rows = query_rows.shape[0]
    log_level = jnp.cumsum(log_gate)
    region = jnp.cumsum(reset_flags)
    row_indices = jnp.arange(block_rows)[:, None]
    col_ids = jnp.arange(block_rows)[None, :]
    inside_segment_mask = (col_ids <= row_indices) & (region[:, None] == region[None, :])
    log_gap = jnp.where(inside_segment_mask, log_level[:, None] - log_level[None, :], 0.0)
    weight = jnp.where(inside_segment_mask, jnp.exp(log_gap), 0.0)
    carried = jnp.where(region == 0, jnp.exp(log_level), 0.0)
    strictly = col_ids < row_indices
    intersection = jnp.dot(key_rows, key_rows.T, precision=highest)
    system = jnp.eye(block_rows, dtype=query_rows.dtype) + jnp.where(
        strictly, write_rate[:, None] * weight * intersection, 0.0
    )
    right_side = jnp.concatenate(
        [write_rate[:, None] * value_rows, (write_rate * carried)[:, None] * key_rows], axis=1
    )
    solved = jax.scipy.linalg.solve_triangular(system, right_side, lower=True, unit_diagonal=True)
    value_width = value_rows.shape[1]
    update = solved[:, :value_width]
    shrink = solved[:, value_width:]
    scores = jnp.dot(query_rows, key_rows.T, precision=highest) * weight
    if not inclusive:
        scores = jnp.where(strictly, scores, 0.0)
    local_out = jnp.dot(scores, update, precision=highest)
    effective = carried[:, None] * query_rows - jnp.dot(scores, shrink, precision=highest)
    trailing_weight = weight[block_rows - 1]
    scaled = trailing_weight[:, None] * key_rows
    transit = carried[block_rows - 1] * jnp.eye(
        key_rows.shape[1], dtype=query_rows.dtype
    ) - jnp.dot(shrink.T, scaled, precision=highest)
    inject = jnp.dot(update.T, scaled, precision=highest)
    return (local_out, effective, transit, inject)


def block_pieces(query_rows, key_rows, value_rows, write_rate, log_gate, reset_flags, inclusive):
    count = query_rows.shape[0] // SPAN

    def split(member):
        return member.reshape((count, SPAN) + member.shape[1:])

    return jax.vmap(partial(span_parts, inclusive=inclusive))(
        split(query_rows),
        split(key_rows),
        split(value_rows),
        split(write_rate),
        split(log_gate),
        split(reset_flags),
    )


def combine(earlier, later):
    highest = lax.Precision.HIGHEST
    return (
        jnp.einsum("hij,hjk->hik", earlier[0], later[0], precision=highest),
        jnp.einsum("hij,hjk->hik", earlier[1], later[0], precision=highest) + later[1],
    )


def summarize(transit, inject):
    heads = transit.shape[0]
    start = (
        jnp.broadcast_to(jnp.eye(DK, dtype=jnp.float32), (heads, DK, DK)),
        jnp.zeros((heads, DV, DK), jnp.float32),
    )

    def step(carry, piece):
        return (combine(carry, piece), None)

    result, unused = lax.scan(
        step, start, (jnp.moveaxis(transit, 1, 0), jnp.moveaxis(inject, 1, 0))
    )
    return result


def emit(local_out, effective, transit, inject, state):
    highest = lax.Precision.HIGHEST
    moved = (
        jnp.moveaxis(local_out, 1, 0),
        jnp.moveaxis(effective, 1, 0),
        jnp.moveaxis(transit, 1, 0),
        jnp.moveaxis(inject, 1, 0),
    )

    def step(carry, piece):
        out_block, effect_rows, transit_step, inject_step = piece
        produced = out_block + jnp.einsum("hck,hvk->hcv", effect_rows, carry, precision=highest)
        carry = jnp.einsum("hvj,hjk->hvk", carry, transit_step, precision=highest) + inject_step
        return (carry, produced)

    final_state, produced = lax.scan(step, state, moved)
    heads = produced.shape[1]
    return jnp.moveaxis(produced, 0, 1).reshape(heads, -1, produced.shape[-1])


def on_device(queries, keys, values, beta, log_decay, seg_lengths):
    highest = lax.Precision.HIGHEST
    query_all, key_all, value_all, rate_all, gate_values_full = (
        lax.all_to_all(queries, "head", split_axis=1, concat_axis=0, tiled=True),
        lax.all_to_all(keys, "head", split_axis=1, concat_axis=0, tiled=True),
        lax.all_to_all(values, "head", split_axis=1, concat_axis=0, tiled=True),
        lax.all_to_all(beta, "head", split_axis=1, concat_axis=0, tiled=True),
        lax.all_to_all(log_decay, "head", split_axis=1, concat_axis=0, tiled=True),
    )
    rows = query_all.shape[0]
    heads = rate_all.shape[1]
    spread = lax.axis_size("seq")
    place = lax.axis_index("seq")
    total = rows * spread
    starts = jnp.cumsum(seg_lengths) - seg_lengths
    positions = place * rows + jnp.arange(rows, dtype=jnp.int32)
    forward_reset = jnp.any(positions[:, None] == starts[None, :], axis=1).astype(jnp.int32)
    backward_reset = (
        jnp.any((positions + 1)[:, None] == starts[None, :], axis=1) | (positions == total - 1)
    ).astype(jnp.int32)

    def by_head(array, width):
        return array.reshape(rows, heads, width).transpose(1, 0, 2).astype(jnp.float32)

    query_heads = by_head(query_all, DK)
    key_raw = by_head(key_all, DK)
    key_heads = key_raw / jnp.sqrt(jnp.sum(key_raw * key_raw, axis=-1, keepdims=True) + 1e-06)
    value_heads = by_head(value_all, DV)
    rate_heads = rate_all.T.astype(jnp.float32)
    gate_heads = gate_values_full.T.astype(jnp.float32)
    forward_pieces = jax.vmap(partial(block_pieces, reset_flags=forward_reset, inclusive=True))(
        query_heads, key_heads, value_heads, rate_heads, gate_heads
    )
    backward_pieces = jax.vmap(
        partial(block_pieces, reset_flags=backward_reset[::-1], inclusive=False)
    )(
        query_heads[:, ::-1],
        key_heads[:, ::-1],
        value_heads[:, ::-1],
        rate_heads[:, ::-1],
        gate_heads[:, ::-1],
    )
    forward_sum = summarize(forward_pieces[2], forward_pieces[3])
    backward_sum = summarize(backward_pieces[2], backward_pieces[3])
    every = (
        lax.all_gather(forward_sum[0][None], "seq", axis=0, tiled=True),
        lax.all_gather(forward_sum[1][None], "seq", axis=0, tiled=True),
        lax.all_gather(backward_sum[0][None], "seq", axis=0, tiled=True),
        lax.all_gather(backward_sum[1][None], "seq", axis=0, tiled=True),
    )
    empty = jnp.zeros_like(forward_sum[1])

    def take_lower(step, state):
        moved = (
            jnp.einsum("hvj,hjk->hvk", state, every[0][step], precision=highest) + every[1][step]
        )
        return jnp.where(step < place, moved, state)

    def take_upper(step, state):
        source = spread - 1 - step
        moved = (
            jnp.einsum("hvj,hjk->hvk", state, every[2][source], precision=highest)
            + every[3][source]
        )
        return jnp.where(source > place, moved, state)

    forward_in = lax.fori_loop(0, spread, take_lower, empty)
    backward_in = lax.fori_loop(0, spread, take_upper, empty)
    forward_out = emit(
        forward_pieces[0], forward_pieces[1], forward_pieces[2], forward_pieces[3], forward_in
    )
    backward_out = emit(
        backward_pieces[0], backward_pieces[1], backward_pieces[2], backward_pieces[3], backward_in
    )[:, ::-1]
    mixed = (
        (forward_out + backward_out)
        .transpose(1, 0, 2)
        .reshape(rows, heads * DV)
        .astype(jnp.bfloat16)
    )
    return lax.all_to_all(mixed, "head", split_axis=0, concat_axis=1, tiled=True)


def solution(mesh):
    in_specs = (
        P(("seq", "head"), None),
        P(("seq", "head"), None),
        P(("seq", "head"), None),
        P(("seq", "head"), None),
        P(("seq", "head"), None),
        P(),
    )
    out_specs = P(("seq", "head"), None)
    devices = mesh.shape["seq"] * mesh.shape["head"]

    def run(queries, keys, values, beta, log_decay, seg_lengths):
        alone = beta.shape[1] == devices and queries.shape[0] == devices * TILE
        return jax.shard_map(
            one_head_each if alone else on_device,
            mesh=mesh,
            in_specs=in_specs,
            out_specs=out_specs,
            check_vma=False,
        )(queries, keys, values, beta, log_decay, seg_lengths)

    return run
```

```python
from functools import partial

import jax
import jax.numpy as jnp
from jax import lax
from jax.experimental import pallas as pl
from jax.experimental.pallas import tpu as pltpu
from jax.sharding import PartitionSpec as P

DK = 128
DV = 128
SPAN = 64
TILE = 128
SIDE = 16
GROUP = 4
LEVELS = 6


def mm(a, b):
    return jnp.dot(a, b, preferred_element_type=jnp.float32)


def halves(a):
    high = a.astype(jnp.bfloat16)
    low = (a - high.astype(jnp.float32)).astype(jnp.bfloat16)
    return high, low


def wide(a):
    return jnp.concatenate(halves(a), axis=1)


def right(high, low):
    row = jnp.concatenate([high, low], axis=1)
    return jnp.concatenate([row, row], axis=0)


def fold(a):
    return a[:, :TILE] + a[:, TILE:]


def mix_kernel(
    spread,
    inner,
    group,
    lengths,
    side_ref,
    q_ref,
    k_ref,
    v_ref,
    out_ref,
    q_all,
    k_all,
    v_all,
    side_all,
    masks,
    fe,
    go,
    partial_out,
    mixed,
    own_sem,
    send_sem,
    recv_sem,
    back_send,
    back_recv,
):
    count = spread * inner
    me = lax.axis_index("seq") * inner + lax.axis_index("head")

    def device(index):
        return (index // inner, index % inner)

    def columns(index):
        return pl.ds(pl.multiple_of(index * TILE, TILE), TILE)

    barrier = pltpu.get_barrier_semaphore()

    def greet(s, carry):
        pl.semaphore_signal(
            barrier,
            inc=1,
            device_id=device((me + s) % count),
            device_id_type=pl.DeviceIdType.MESH,
        )
        return carry

    lax.fori_loop(1, count, greet, 0)
    pl.semaphore_wait(barrier, count - 1)

    def pairs(head, block):
        return (
            (side_ref.at[head], side_all.at[block]),
            (k_ref.at[:, columns(head)], k_all.at[block]),
            (v_ref.at[:, columns(head)], v_all.at[block]),
            (q_ref.at[:, columns(head)], q_all.at[block]),
        )

    def sends(target, source):
        return [
            pltpu.make_async_remote_copy(
                src_ref=src,
                dst_ref=dst,
                send_sem=send_sem.at[kind, target],
                recv_sem=recv_sem.at[kind, source],
                device_id=device(target),
                device_id_type=pl.DeviceIdType.MESH,
            )
            for kind, (src, dst) in enumerate(pairs(target, source))
        ]

    def give(s, carry):
        for copy in sends((me + s) % count, me):
            copy.start()
        return carry

    lax.fori_loop(1, count, give, 0)
    own = [
        pltpu.make_async_copy(src, dst, own_sem.at[kind])
        for kind, (src, dst) in enumerate(pairs(me, me))
    ]
    for copy in own:
        copy.start()

    bf16, f32 = jnp.bfloat16, jnp.float32
    rows = lax.broadcasted_iota(jnp.int32, (TILE, TILE), 0)
    cols = lax.broadcasted_iota(jnp.int32, (TILE, TILE), 1)
    rows_w = lax.broadcasted_iota(jnp.int32, (TILE, 2 * TILE), 0)
    cols_w = lax.broadcasted_iota(jnp.int32, (TILE, 2 * TILE), 1) & (TILE - 1)
    for level in range(1, LEVELS + 1):
        hit = ((rows_w ^ cols_w) >> level) == 1
        masks[level - 1] = jnp.where(hit, 1.0, 0.0).astype(f32).astype(bf16)
    starts = []
    total = jnp.int32(0)
    for s in range(lengths.shape[0]):
        starts.append(total)
        total = total + lengths[s]

    def segment_of(position):
        seg = jnp.zeros_like(position)
        for s in starts:
            seg = seg + jnp.where(position >= s, 1, 0)
        return seg

    for copy in own:
        copy.wait()

    def prepare(g, carry):
        for m in range(group):
            s = g * group + m

            @pl.when(s > 0)
            def _():
                source = (me + count - s) % count
                for copy in sends(source, source):
                    copy.wait_recv()

        eye = jnp.where(rows == cols, 1.0, 0.0).astype(f32)
        ramp = jnp.where(rows <= cols, 1.0, 0.0).astype(f32).astype(bf16)
        near = (rows ^ cols) == 1
        chains = []
        for m in range(group):
            c = (me + count - (g * group + m)) % count
            q, k, v, side32 = q_all[c], k_all[c], v_all[c], side_all[c]
            k_t = k.astype(f32).T.astype(bf16)
            both = mm(jnp.concatenate([q, k], axis=0), k_t)
            qk, kk = both[:TILE], both[TILE:]
            b_row, g_row = side32[0:1], side32[1:2]
            level = mm(jnp.concatenate([side32] * (SIDE // 2), axis=0).astype(bf16), ramp)
            inc_row = level[1:2]
            exc_row = inc_row - g_row
            base = c * TILE
            position = base + lax.broadcasted_iota(jnp.int32, (1, TILE), 1)
            seg_row = segment_of(position).astype(f32)
            before = segment_of(base - 1).astype(f32)
            after = jnp.where(c == count - 1, -1, segment_of(base + TILE)).astype(f32)
            stacked = jnp.concatenate(
                [inc_row, exc_row, b_row, seg_row, jnp.zeros((4, TILE), f32)], axis=0
            )
            stacked_t = stacked.T
            inc_col, exc_col = stacked_t[:, 0:1], stacked_t[:, 1:2]
            b_col, seg_col = stacked_t[:, 2:3], stacked_t[:, 3:4]
            diagonal = kk * eye
            rn_row = 1.0 / jnp.sqrt(jnp.sum(diagonal, axis=0, keepdims=True) + 1e-06)
            rn_col = 1.0 / jnp.sqrt(jnp.sum(diagonal, axis=1, keepdims=True) + 1e-06)
            same = seg_col == seg_row
            kk_b = kk * (rn_col * b_col) * rn_row
            qk_n = qk * rn_row
            last_inc = inc_row[:, TILE - 1 : TILE]
            last_seg = seg_row[:, TILE - 1 : TILE]
            first_seg = seg_row[:, 0:1]
            v2 = jnp.concatenate([v, v], axis=0)
            k2 = jnp.concatenate([k, k], axis=0)
            kt2 = jnp.concatenate([k_t, k_t], axis=1)
            q32 = q.astype(f32)
            for direction in range(2):
                if direction == 0:
                    inside = same & (cols <= rows)
                    strict = cols < rows
                    gap = inc_col - inc_row
                    c_row = jnp.where(seg_row == before, jnp.exp(inc_row), 0.0)
                    c_col = jnp.where(seg_col == before, jnp.exp(inc_col), 0.0)
                    w_col = jnp.where(seg_col == last_seg, jnp.exp(last_inc - inc_col), 0.0)
                    c_last = c_row[:, TILE - 1 : TILE]
                else:
                    inside = same & (cols >= rows)
                    strict = cols > rows
                    gap = exc_row - exc_col
                    c_row = jnp.where(seg_row == after, jnp.exp(last_inc - exc_row), 0.0)
                    c_col = jnp.where(seg_col == after, jnp.exp(last_inc - exc_col), 0.0)
                    w_col = jnp.where(seg_col == first_seg, jnp.exp(exc_col), 0.0)
                    c_last = c_row[:, 0:1]
                weight = jnp.where(inside, jnp.exp(jnp.where(inside, gap, 0.0)), 0.0)
                lower = jnp.where(strict, weight * kk_b, 0.0)
                scores = weight * qk_n
                if direction == 1:
                    scores = jnp.where(strict, scores, 0.0)
                chains.append(
                    dict(
                        place=2 * c + direction,
                        lower=wide(lower),
                        inverse=eye - jnp.where(near, lower, 0.0),
                        scores=halves(scores),
                        b_row=b_row,
                        bc_row=b_row * c_row * rn_row,
                        wn_col=w_col * rn_col,
                        c_last=c_last,
                        cq=c_col * q32,
                        v2=v2,
                        k2=k2,
                        kt2=kt2,
                    )
                )
        for level in range(LEVELS):
            mask = masks[level]
            parts = [halves(n["inverse"]) for n in chains]
            inner = [fold(mm(n["lower"] * mask, right(*p))) for n, p in zip(chains, parts)]
            outer = [
                fold(mm(jnp.concatenate(p, axis=1), right(*halves(y))))
                for p, y in zip(parts, inner)
            ]
            for n, y in zip(chains, outer):
                n["inverse"] = n["inverse"] - y
        solved = [
            jnp.concatenate(
                [
                    mm(wide(n["inverse"] * n["b_row"]), n["v2"]),
                    mm(wide(n["inverse"] * n["bc_row"]), n["k2"]),
                ],
                axis=1,
            )
            for n in chains
        ]
        for n, u in zip(chains, solved):
            u_h, u_l = halves(u)
            s_h, s_l = n["scores"]
            seen = mm(jnp.concatenate([s_h, s_l], axis=1), jnp.concatenate([u_h, u_h], axis=0))
            seen = seen + mm(s_h, u_l)
            kept = mm(n["kt2"], jnp.concatenate(halves(u * n["wn_col"]), axis=0))
            effect = n["cq"] - seen[:, TILE:]
            transit = n["c_last"] * eye - kept[:, TILE:]
            fe[n["place"]] = wide(jnp.concatenate([transit, effect], axis=0))
            go[n["place"]] = jnp.concatenate([kept[:, :TILE], seen[:, :TILE]], axis=0)
        return carry

    lax.fori_loop(0, count // group, prepare, 0)

    def advance(turn, states):
        for m in range(group):
            step = turn * group + m
            later = []
            for direction, state in enumerate(states):
                c = step if direction == 0 else count - 1 - step
                place = 2 * c + direction
                moved = fold(mm(fe[place], right(*halves(state)))) + go[place]
                partial_out[place] = moved[TILE:]
                later.append(moved[:TILE])
            states = tuple(later)
        return states

    empty = jnp.zeros((TILE, TILE), f32)
    lax.fori_loop(0, count // group, advance, (empty, empty))

    def returns(target, source):
        return pltpu.make_async_remote_copy(
            src_ref=mixed.at[target],
            dst_ref=out_ref.at[:, columns(source)],
            send_sem=back_send.at[target],
            recv_sem=back_recv.at[source],
            device_id=device(target),
            device_id_type=pl.DeviceIdType.MESH,
        )

    def finish(s, carry):
        c = (me + s) % count
        mixed[c] = (partial_out[2 * c] + partial_out[2 * c + 1]).astype(bf16)
        returns(c, me).start()
        return carry

    lax.fori_loop(1, count, finish, 0)
    out_ref[:, columns(me)] = (partial_out[2 * me] + partial_out[2 * me + 1]).astype(bf16)

    def settle(s, carry):
        target = (me + s) % count
        for copy in sends(target, me):
            copy.wait_send()
        returns(target, me).wait_send()
        source = (me + count - s) % count
        returns(source, source).wait_recv()
        return carry

    lax.fori_loop(1, count, settle, 0)


def one_head_each(queries, keys, values, beta, log_decay, seg_lengths):
    spread, inner = lax.axis_size("seq"), lax.axis_size("head")
    count = spread * inner
    group = GROUP if count % GROUP == 0 else 1
    side = jnp.stack([beta.T, log_decay.T], axis=1)
    side = side.astype(jnp.float32)
    return pl.pallas_call(
        partial(mix_kernel, spread, inner, group),
        out_shape=jax.ShapeDtypeStruct((TILE, count * DV), jnp.bfloat16),
        in_specs=[pl.BlockSpec(memory_space=pltpu.SMEM)]
        + [pl.BlockSpec(memory_space=pltpu.VMEM)]
        + [pl.BlockSpec(memory_space=pl.ANY)] * 3,
        out_specs=pl.BlockSpec(memory_space=pltpu.VMEM),
        scratch_shapes=[
            pltpu.VMEM((count, TILE, DK), jnp.bfloat16),
            pltpu.VMEM((count, TILE, DK), jnp.bfloat16),
            pltpu.VMEM((count, TILE, DV), jnp.bfloat16),
            pltpu.VMEM((count, 2, TILE), jnp.float32),
            pltpu.VMEM((LEVELS, TILE, 2 * TILE), jnp.bfloat16),
            pltpu.VMEM((2 * count, 2 * TILE, 2 * TILE), jnp.bfloat16),
            pltpu.VMEM((2 * count, 2 * TILE, TILE), jnp.float32),
            pltpu.VMEM((2 * count, TILE, TILE), jnp.float32),
            pltpu.VMEM((count, TILE, DV), jnp.bfloat16),
            pltpu.SemaphoreType.DMA((4,)),
            pltpu.SemaphoreType.DMA((4, count)),
            pltpu.SemaphoreType.DMA((4, count)),
            pltpu.SemaphoreType.DMA((count,)),
            pltpu.SemaphoreType.DMA((count,)),
        ],
        compiler_params=pltpu.CompilerParams(
            collective_id=0, has_side_effects=True, vmem_limit_bytes=52 * 1024 * 1024
        ),
        cost_estimate=pl.CostEstimate(
            flops=count * 40 * TILE * 512 * 256, bytes_accessed=count * 131072, transcendentals=0
        ),
    )(seg_lengths, side, queries, keys, values)


def span_parts(query_rows, key_rows, value_rows, write_rate, log_gate, reset_flags, inclusive):
    highest = lax.Precision.HIGHEST
    block_rows = query_rows.shape[0]
    log_level = jnp.cumsum(log_gate)
    region = jnp.cumsum(reset_flags)
    row_indices = jnp.arange(block_rows)[:, None]
    col_ids = jnp.arange(block_rows)[None, :]
    inside_segment_mask = (col_ids <= row_indices) & (region[:, None] == region[None, :])
    log_gap = jnp.where(inside_segment_mask, log_level[:, None] - log_level[None, :], 0.0)
    weight = jnp.where(inside_segment_mask, jnp.exp(log_gap), 0.0)
    carried = jnp.where(region == 0, jnp.exp(log_level), 0.0)
    strictly = col_ids < row_indices
    intersection = jnp.dot(key_rows, key_rows.T, precision=highest)
    system = jnp.eye(block_rows, dtype=query_rows.dtype) + jnp.where(
        strictly, write_rate[:, None] * weight * intersection, 0.0
    )
    right_side = jnp.concatenate(
        [write_rate[:, None] * value_rows, (write_rate * carried)[:, None] * key_rows], axis=1
    )
    solved = jax.scipy.linalg.solve_triangular(system, right_side, lower=True, unit_diagonal=True)
    value_width = value_rows.shape[1]
    update = solved[:, :value_width]
    shrink = solved[:, value_width:]
    scores = jnp.dot(query_rows, key_rows.T, precision=highest) * weight
    if not inclusive:
        scores = jnp.where(strictly, scores, 0.0)
    local_out = jnp.dot(scores, update, precision=highest)
    effective = carried[:, None] * query_rows - jnp.dot(scores, shrink, precision=highest)
    trailing_weight = weight[block_rows - 1]
    scaled = trailing_weight[:, None] * key_rows
    transit = carried[block_rows - 1] * jnp.eye(
        key_rows.shape[1], dtype=query_rows.dtype
    ) - jnp.dot(shrink.T, scaled, precision=highest)
    inject = jnp.dot(update.T, scaled, precision=highest)
    return (local_out, effective, transit, inject)


def block_pieces(query_rows, key_rows, value_rows, write_rate, log_gate, reset_flags, inclusive):
    count = query_rows.shape[0] // SPAN

    def split(member):
        return member.reshape((count, SPAN) + member.shape[1:])

    return jax.vmap(partial(span_parts, inclusive=inclusive))(
        split(query_rows),
        split(key_rows),
        split(value_rows),
        split(write_rate),
        split(log_gate),
        split(reset_flags),
    )


def combine(earlier, later):
    highest = lax.Precision.HIGHEST
    return (
        jnp.einsum("hij,hjk->hik", earlier[0], later[0], precision=highest),
        jnp.einsum("hij,hjk->hik", earlier[1], later[0], precision=highest) + later[1],
    )


def summarize(transit, inject):
    heads = transit.shape[0]
    start = (
        jnp.broadcast_to(jnp.eye(DK, dtype=jnp.float32), (heads, DK, DK)),
        jnp.zeros((heads, DV, DK), jnp.float32),
    )

    def step(carry, piece):
        return (combine(carry, piece), None)

    result, unused = lax.scan(
        step, start, (jnp.moveaxis(transit, 1, 0), jnp.moveaxis(inject, 1, 0))
    )
    return result


def emit(local_out, effective, transit, inject, state):
    highest = lax.Precision.HIGHEST
    moved = (
        jnp.moveaxis(local_out, 1, 0),
        jnp.moveaxis(effective, 1, 0),
        jnp.moveaxis(transit, 1, 0),
        jnp.moveaxis(inject, 1, 0),
    )

    def step(carry, piece):
        out_block, effect_rows, transit_step, inject_step = piece
        produced = out_block + jnp.einsum("hck,hvk->hcv", effect_rows, carry, precision=highest)
        carry = jnp.einsum("hvj,hjk->hvk", carry, transit_step, precision=highest) + inject_step
        return (carry, produced)

    final_state, produced = lax.scan(step, state, moved)
    heads = produced.shape[1]
    return jnp.moveaxis(produced, 0, 1).reshape(heads, -1, produced.shape[-1])


def on_device(queries, keys, values, beta, log_decay, seg_lengths):
    highest = lax.Precision.HIGHEST
    query_all, key_all, value_all, rate_all, gate_values_full = (
        lax.all_to_all(queries, "head", split_axis=1, concat_axis=0, tiled=True),
        lax.all_to_all(keys, "head", split_axis=1, concat_axis=0, tiled=True),
        lax.all_to_all(values, "head", split_axis=1, concat_axis=0, tiled=True),
        lax.all_to_all(beta, "head", split_axis=1, concat_axis=0, tiled=True),
        lax.all_to_all(log_decay, "head", split_axis=1, concat_axis=0, tiled=True),
    )
    rows = query_all.shape[0]
    heads = rate_all.shape[1]
    spread = lax.axis_size("seq")
    place = lax.axis_index("seq")
    total = rows * spread
    starts = jnp.cumsum(seg_lengths) - seg_lengths
    positions = place * rows + jnp.arange(rows, dtype=jnp.int32)
    forward_reset = jnp.any(positions[:, None] == starts[None, :], axis=1).astype(jnp.int32)
    backward_reset = (
        jnp.any((positions + 1)[:, None] == starts[None, :], axis=1) | (positions == total - 1)
    ).astype(jnp.int32)

    def by_head(array, width):
        return array.reshape(rows, heads, width).transpose(1, 0, 2).astype(jnp.float32)

    query_heads = by_head(query_all, DK)
    key_raw = by_head(key_all, DK)
    key_heads = key_raw / jnp.sqrt(jnp.sum(key_raw * key_raw, axis=-1, keepdims=True) + 1e-06)
    value_heads = by_head(value_all, DV)
    rate_heads = rate_all.T.astype(jnp.float32)
    gate_heads = gate_values_full.T.astype(jnp.float32)
    forward_pieces = jax.vmap(partial(block_pieces, reset_flags=forward_reset, inclusive=True))(
        query_heads, key_heads, value_heads, rate_heads, gate_heads
    )
    backward_pieces = jax.vmap(
        partial(block_pieces, reset_flags=backward_reset[::-1], inclusive=False)
    )(
        query_heads[:, ::-1],
        key_heads[:, ::-1],
        value_heads[:, ::-1],
        rate_heads[:, ::-1],
        gate_heads[:, ::-1],
    )
    forward_sum = summarize(forward_pieces[2], forward_pieces[3])
    backward_sum = summarize(backward_pieces[2], backward_pieces[3])
    every = (
        lax.all_gather(forward_sum[0][None], "seq", axis=0, tiled=True),
        lax.all_gather(forward_sum[1][None], "seq", axis=0, tiled=True),
        lax.all_gather(backward_sum[0][None], "seq", axis=0, tiled=True),
        lax.all_gather(backward_sum[1][None], "seq", axis=0, tiled=True),
    )
    empty = jnp.zeros_like(forward_sum[1])

    def take_lower(step, state):
        moved = (
            jnp.einsum("hvj,hjk->hvk", state, every[0][step], precision=highest) + every[1][step]
        )
        return jnp.where(step < place, moved, state)

    def take_upper(step, state):
        source = spread - 1 - step
        moved = (
            jnp.einsum("hvj,hjk->hvk", state, every[2][source], precision=highest)
            + every[3][source]
        )
        return jnp.where(source > place, moved, state)

    forward_in = lax.fori_loop(0, spread, take_lower, empty)
    backward_in = lax.fori_loop(0, spread, take_upper, empty)
    forward_out = emit(
        forward_pieces[0], forward_pieces[1], forward_pieces[2], forward_pieces[3], forward_in
    )
    backward_out = emit(
        backward_pieces[0], backward_pieces[1], backward_pieces[2], backward_pieces[3], backward_in
    )[:, ::-1]
    mixed = (
        (forward_out + backward_out)
        .transpose(1, 0, 2)
        .reshape(rows, heads * DV)
        .astype(jnp.bfloat16)
    )
    return lax.all_to_all(mixed, "head", split_axis=0, concat_axis=1, tiled=True)


def solution(mesh):
    in_specs = (
        P(("seq", "head"), None),
        P(("seq", "head"), None),
        P(("seq", "head"), None),
        P(("seq", "head"), None),
        P(("seq", "head"), None),
        P(),
    )
    out_specs = P(("seq", "head"), None)
    devices = mesh.shape["seq"] * mesh.shape["head"]

    def run(queries, keys, values, beta, log_decay, seg_lengths):
        alone = beta.shape[1] == devices and queries.shape[0] == devices * TILE
        return jax.shard_map(
            one_head_each if alone else on_device,
            mesh=mesh,
            in_specs=in_specs,
            out_specs=out_specs,
            check_vma=False,
        )(queries, keys, values, beta, log_decay, seg_lengths)

    return run
```
